128 devices in a mesh: grp: 8 (over z_lo, x), tp: 16 (over z_hi, y, core).
Axes of the slice: x: 4, y: 4, z: 4 (z_hi: 2, z_lo: 2; z = z_hi * 2 + z_lo), core: 2. Of those that a mesh axis runs over, the one named last changes fastest.
Arguments:
- master: float32 [16, 720, 3, 2880], P('grp', 'tp'), may hold values from -0.109375 to 0.109375
- moment_one: float32 [16, 720, 3, 2880], P('grp', 'tp'), may hold values from -0.06 to 0.06
- moment_two: float32 [16, 720, 3, 2880], P('grp', 'tp'), may hold values from 1e-06 to 0.0001
- gradient: float32 [16, 720, 3, 2880], P('grp', 'tp'), may hold values from -0.3 to 0.3
- piece_owner: int32 [16], replicated, may hold values from 0 to 15, each once
- tokens: bfloat16 [4, 1024, 2880], P(None, 'grp', 'tp'), may hold values from -6 to 6
- routes: int32 [4, 1024, 2], P(None, 'grp'), may hold values from 0 to 3, all different within a row; in each aligned block of 128 rows (0 to 127, 128 to 255, ..., all dimensions but the last counted through in order) at most 96 rows name the same one
- mix_weight: float32 [4, 1024, 2], P(None, 'grp'), may hold values from 0.2 to 1
Outputs:
- decoded: bfloat16 [4, 1024, 2880], P(None, 'grp', 'tp')
The draws below stay inside these ranges and needn't reach their ends.
Inputs may be any that keep to these rules, and one draw needn't show every extreme that they name: `routes`: within each aligned block of 128 rows (one step of one replica) the two choices of a token differ, and no expert is named more than 96 times; some expert is named exactly 96 times. A permutation; piece slot g stores row block piece_owner[g] % 4 of expert piece_owner[g] // 4.
All inputs are finite; a program needn't handle non-finite values.
Results may differ from the reference program's by a relative error of at most 0.0049.
The reference program's roundings to bfloat16 on the way (of `updated`, `weights` and `hidden`) count: a program that leaves them out, or rounds other values in their place, can miss the bound.
Values may be sent and summed in bfloat16 or wider, within the bound.
No kernel may reach another device: no remote copies, remote signals or barrier semaphores. Data moves between devices by JAX's collectives and lax.ppermute only.
A program may use at most 192 MiB of HBM per device.

```python
import math
import jax
import jax.numpy as jnp
import numpy as np
from jax import lax

D = 2880
FF = 2880
EXPERTS = 4
TOP = 2
STEPS = 4
TOK = 128
CAP = 96
PROWS = 720
PIECES = 16
TOKENS = 1024
N_GRP = 8


def block_scale(own_key, dims, cuts, smallest, top_value):
    gain = 1.0
    for axis_at, shards_of in cuts:
        draws = jax.random.uniform(jax.random.fold_in(jax.random.fold_in(own_key, 6), axis_at), (shards_of,), jnp.float32, smallest / len(cuts), top_value / len(cuts))
        gain = gain * jnp.repeat(jnp.exp(draws), dims[axis_at] // shards_of).reshape((-1,) + (1,) * (len(dims) - 1 - axis_at))
    return gain


def shared_out(key, own, number, rows, number_of, top, limit, slope):
    sequence = jax.random.permutation(key, number_of)
    packed, ordinary = portions_of(number_of, rows * top, limit, slope, True), portions_of(number_of, rows * top, limit, slope, False)
    places = jnp.arange(number_of)

    def named(sizes, turn):
        used = int((sizes > 0).sum())
        fixed = max(1, used // 4)
        moved = fixed + (places - fixed + turn * (used - fixed)) % max(1, number_of - fixed)
        return jnp.zeros((number_of,), jnp.int32).at[sequence[jnp.where(places < fixed, places, moved)]].set(jnp.asarray(sizes, jnp.int32))

    sizes = jnp.where(number % 4 == 0, named(packed, number // 4), named(ordinary, number - number // 4 - 1))
    mixed = jax.random.permutation(jax.random.fold_in(own, 3), number_of)
    giver, sink = mixed[0:number_of // 2 * 2:2], mixed[1:number_of // 2 * 2:2]
    room = jnp.minimum(sizes[giver] - 1, limit - sizes[sink]) // 2
    room = jnp.where((giver == sequence[0]) | (sink == sequence[0]) | (sizes[sink] == 0), 0, jnp.maximum(room, 0))
    moved = jax.random.randint(jax.random.fold_in(own, 4), (number_of // 2,), 0, 1 << 20) % (room + 1)
    sizes = sizes.at[giver].add(-moved).at[sink].add(moved)
    labels = jnp.searchsorted(jnp.cumsum(sizes), jnp.arange(rows * top), side="right").astype(jnp.int32)
    table = labels.reshape(top, rows).T
    table = table[jax.random.permutation(jax.random.fold_in(own, 1), rows)]
    turn = jax.random.randint(jax.random.fold_in(own, 2), (rows, 1), 0, top)
    return jnp.take_along_axis(table, (jnp.arange(top)[None, :] + turn) % top, axis=1)


def portions_of(count, total, limit, skew, full):
    weights = [(1 << 20) // math.isqrt(grade ** skew) + 1 for grade in range(1, count + 1)]
    largest = limit if full else min(limit, max(-(-total // count), total * weights[0] // sum(weights)))
    least = 1 if total - largest >= count - 1 else 0
    counts, surplus = [largest] + [least] * (count - 1), total - largest - least * (count - 1)
    while surplus > 0:
        candidates = [i for i in range(1, count) if counts[i] < largest] or [i for i in range(1, count) if counts[i] < limit]
        whole, budget = sum([weights[i] for i in candidates]), surplus
        for i in candidates:
            extra = min(limit - counts[i], max(1, budget * weights[i] // whole), surplus)
            counts[i] = counts[i] + extra
            surplus = surplus - extra
    return np.array(counts)


def bell_draw(own_key, shape, spread, limit, shards=(), kind=jnp.bfloat16):
    values = jax.random.normal(own_key, shape, jnp.float32) * spread
    if len(shards) > 0:
        values = block_scale(own_key, shape, shards, -0.22, 0.18) * values
    return jnp.clip(values, min=-limit, max=limit).astype(kind)


def setup_inputs(seed: int = 0) -> dict:
    keys = jax.random.split(jax.random.key(seed), 9)
    master = bell_draw(keys[0], (PIECES, PROWS, 3, FF), D ** -0.5, 0.109375, ((0, 8), (1, 16)), jnp.float32)
    moment_one = bell_draw(keys[1], (PIECES, PROWS, 3, FF), 0.01, 0.06, ((0, 8), (1, 16)), jnp.float32)
    moment_two = jnp.clip(jnp.exp(math.log(0.0001) - 4.6051702 * jax.random.uniform(keys[2], (PIECES, PROWS, 3, FF), jnp.float32) ** block_scale(keys[2], (PIECES, PROWS, 3, FF), ((0, 8), (1, 16)), -0.2, 0.2)), 9.999999974752427e-07, 0.0001)
    gradient = bell_draw(keys[3], (PIECES, PROWS, 3, FF), 0.05, 0.3, ((0, 8), (1, 16)), jnp.float32)
    piece_owner = jax.random.permutation(keys[4], PIECES).astype(jnp.int32)
    tokens = bell_draw(keys[5], (STEPS, TOKENS, D), 1.0, 6.0, ((1, 8), (2, 16)))
    routes_keys = jax.random.split(jax.random.fold_in(keys[6], 1), STEPS * TOKENS // TOK)
    routes_turns = jax.random.permutation(jax.random.fold_in(keys[6], 3), STEPS * TOKENS // TOK)
    routes = jax.vmap(lambda own, number: shared_out(jax.random.fold_in(keys[6], 2), own, number, TOK, EXPERTS, TOP, CAP, 2))(routes_keys, routes_turns).reshape((STEPS, TOKENS, TOP))
    mix_weight = jnp.clip(0.2 + 0.8 * jax.random.uniform(keys[7], (STEPS, TOKENS, TOP), jnp.float32) ** block_scale(keys[7], (STEPS, TOKENS, TOP), ((1, 8),), -0.2, 0.2), 0.2, 1.0)
    return dict(master=master, moment_one=moment_one, moment_two=moment_two, gradient=gradient, piece_owner=piece_owner, tokens=tokens, routes=routes, mix_weight=mix_weight)


learn_rate = 0.003
beta_one = 0.9
beta_two = 0.999
adam_eps = 1e-08
decay_rate = 0.1
bias_one = 1.0 - 0.9 ** 20
bias_two = 1.0 - 0.999 ** 20

def dispatch(chosen, experts, capacity):
    token_count, top_count = chosen.shape
    chosen_flat = chosen.reshape(-1)
    one_hot = (chosen_flat[:, None] == jnp.arange(experts, dtype=jnp.int32)[None, :]).astype(jnp.int32)
    earlier = jnp.cumsum(one_hot, axis=0, dtype=jnp.int32) - one_hot
    slot_of = lax.optimization_barrier(jnp.sum(earlier * one_hot, axis=1, dtype=jnp.int32))
    slot_ids = (chosen_flat * capacity + slot_of).astype(jnp.int32)
    owner_rows = (jnp.arange(token_count * top_count, dtype=jnp.int32) // top_count).astype(jnp.int32)
    source_rows = jnp.zeros((experts * capacity,), jnp.int32).at[slot_ids].set(owner_rows)
    return (slot_ids, source_rows)

def reference(master, moment_one, moment_two, gradient, piece_owner, tokens, routes, mix_weight):
    moment_new = beta_one * moment_one + (1.0 - beta_one) * gradient
    second_new = beta_two * moment_two + (1.0 - beta_two) * gradient * gradient
    adjust = moment_new / bias_one / (jnp.sqrt(second_new / bias_two) + adam_eps) + decay_rate * master
    updated = (master - learn_rate * adjust).astype(jnp.bfloat16)
    piece_count = piece_owner.shape[0]
    inverse = jnp.zeros((piece_count,), jnp.int32).at[piece_owner].set(jnp.arange(piece_count, dtype=jnp.int32))
    ordered = jnp.take(updated, inverse, axis=0)
    wide_weights = ordered.reshape(EXPERTS, D, 3, FF).astype(jnp.float32)
    gate_up_weight = wide_weights[:, :, 0:2, :]
    down_weight = wide_weights[:, :, 2, :]

    def moe_block(inputs):
        token_rows, chosen, mixing = inputs
        slot_ids, source_rows = dispatch(chosen, EXPERTS, CAP)
        picked = jnp.take(token_rows, source_rows, axis=0).reshape(EXPERTS, CAP, D).astype(jnp.float32)
        gate_up_out = jnp.einsum('ecd,edkf->eckf', picked, gate_up_weight, precision=lax.Precision.HIGHEST)
        gate = gate_up_out[:, :, 0, :]
        upper = gate_up_out[:, :, 1, :]
        hidden = ((upper + 1.0) * gate * jax.nn.sigmoid(1.702 * gate)).astype(jnp.bfloat16)
        hidden = lax.optimization_barrier(hidden).astype(jnp.float32)
        expert_out = jnp.einsum('ecf,edf->ecd', hidden, down_weight, precision=lax.Precision.HIGHEST)
        gathered = jnp.take(expert_out.reshape(EXPERTS * CAP, D), slot_ids, axis=0)
        combined = lax.optimization_barrier(jnp.sum(gathered.reshape(TOK, TOP, D) * mixing[:, :, None], axis=1))
        return combined.astype(jnp.bfloat16)
    blocks = STEPS * N_GRP
    results = lax.map(moe_block, (tokens.reshape(blocks, TOK, D), routes.reshape(blocks, TOK, TOP), mix_weight.reshape(blocks, TOK, TOP)))
    return results.reshape(STEPS, TOKENS, D)
```

```python
import functools

import jax
import jax.numpy as jnp
from jax import lax
from jax.experimental import pallas as pl
from jax.experimental.pallas import tpu as pltpu
from jax.sharding import Mesh
from jax.sharding import PartitionSpec as P

EXPERTS = 4
ROWS = 48
TOK = 512

learn_rate = 0.003
beta_one = 0.9
beta_two = 0.999
adam_eps = 1e-08
decay_rate = 0.1
bias_one = 1.0 - 0.9**20
bias_two = 1.0 - 0.999**20

bf16 = jnp.bfloat16
f32 = jnp.float32


def pack_kernel(w_ref, o_ref):
    lane = lax.broadcasted_iota(jnp.int32, (ROWS, 128), 1)

    def load(s, k, j):
        return w_ref[s, k, :, j * 128 : (j + 1) * 128].astype(f32)

    def roll(x, by):
        by = by % 128
        return x if by == 0 else pltpu.roll(x, by, 1)

    for j in range(8):
        for s in range(2):
            gate_b, up_b = load(s, 0, 16 + j), load(s, 1, 16 + j)
            for half in range(2):
                i = 2 * j + half
                gate, up, down = load(s, 0, i), load(s, 1, i), load(s, 2, i)
                for odd in range(2):
                    d = 2 * i + odd
                    off = 32 * (d % 4)
                    first = jnp.where(lane < 64, roll(gate, 64 * odd), roll(up, 64 - 64 * odd))
                    o_ref[d, 2 * s] = first.astype(bf16)
                    rest = jnp.where(lane < 96, roll(gate_b, 64 - off), roll(up_b, 96 - off))
                    second = jnp.where(lane < 64, roll(down, 64 * odd), rest)
                    o_ref[d, 2 * s + 1] = second.astype(bf16)
        down_0, down_1 = load(0, 2, 16 + j), load(1, 2, 16 + j)
        for q in range(4):
            last = jnp.where(lane < 32, roll(down_0, -32 * q), roll(down_1, 32 - 32 * q))
            o_ref[4 * j + q, 4] = jnp.where(lane < 64, last, 0.0).astype(bf16)


def expert_kernel(tab, mix_ref, x_ref, w0, w1a, w1b, w2a, w2b, w3a, w3b, own_ref, send_ref, wbuf, dbuf, acc, hid, out):
    sources = ((w0, 0), (w0, 16), (w1a, 0), (w1b, 0), (w2a, 0), (w2b, 0), (w3a, 0), (w3b, 0))
    lane = lax.broadcasted_iota(jnp.int32, (2 * TOK, 128), 1)

    def fill(i, parts):
        src, slot = tab[2 * i], tab[2 * i + 1]
        for n, (ref, at) in enumerate(sources):

            @pl.when(src == n)
            def _():
                for to, col, tile in parts:
                    which = 4 if tile is None else 2 * slot + tile
                    for t in range(16):
                        to[t * ROWS : (t + 1) * ROWS, col : col + 128] = ref[at + t, which]

        return slot

    @pl.loop(0, EXPERTS)
    def _(e):
        @pl.loop(0, 4)
        def _(b):
            fill(4 * e + b, ((wbuf, 0, 0), (wbuf, 128, 1)))
            part = jnp.dot(x_ref[b], wbuf[...], preferred_element_type=f32)

            @pl.when(b == 0)
            def _():
                acc[...] = part

            @pl.when(b > 0)
            def _():
                acc[...] += part

        first = acc[:, 0:128]
        hidden_a = (pltpu.roll(first, 64, 1) + 1.0) * first * jax.nn.sigmoid(1.702 * first)
        rest = acc[:, 128:256]
        gate = pltpu.roll(rest, 64, 1)
        hidden_b = (pltpu.roll(rest, 32, 1) + 1.0) * gate * jax.nn.sigmoid(1.702 * gate)
        hidden_a = jnp.where(lane < 64, hidden_a, 0.0).astype(bf16)
        hidden_b = jnp.where(lane < 32, hidden_b, 0.0)
        hid[e, 0, :, 0:128] = hidden_a
        hid[e, 1, :, 0:128] = hidden_a
        hid[e, 0, :, 128:256] = hidden_b.astype(bf16)
        hid[e, 1, :, 128:256] = pltpu.roll(hidden_b, 32, 1).astype(bf16)

    core = tab[32]

    @pl.loop(0, 4)
    def _(b):
        @pl.loop(0, EXPERTS)
        def _(e):
            slot = fill(4 * e + b, ((dbuf, 0, 1), (dbuf, 128, None)))
            part = lax.dot_general(
                dbuf[...], hid[e, slot], (((1,), (1,)), ((), ())), preferred_element_type=f32
            )
            part = part * mix_ref[pl.ds(e, 1), :]

            @pl.when(e == 0)
            def _():
                out[...] = part

            @pl.when(e > 0)
            def _():
                out[...] += part

        for q in range(4):
            block = out[q * 192 : (q + 1) * 192, :].astype(bf16)

            @pl.when(core == q % 2)
            def _():
                for z in range(2):
                    own_ref[8 * z + 2 * b + q // 2] = block[:, z * TOK : (z + 1) * TOK]

            @pl.when(core != q % 2)
            def _():
                for z in range(2):
                    send_ref[8 * z + 2 * b + q // 2] = block[:, z * TOK : (z + 1) * TOK]


def shards(master, moment_one, moment_two, gradient, piece_owner, tokens, routes, mix_weight):
    xi, zl, core = lax.axis_index("x"), lax.axis_index("zl"), lax.axis_index("core")
    plane = ("zl", "zh", "y", "core")

    own_x = tokens.transpose(2, 0, 1).reshape(4, 45, TOK)
    own_x = jnp.pad(own_x, ((0, 0), (0, ROWS - 45), (0, 0))).reshape(4 * ROWS, TOK)
    every_x = lax.all_gather(own_x, plane)
    x_all = every_x.reshape(2, 4, 768, TOK).transpose(1, 0, 3, 2).reshape(4, 2 * TOK, 768)

    flat_routes = routes.reshape(TOK, 2)
    flat_mix = mix_weight.reshape(TOK, 2)
    mine = jnp.sum(
        jnp.where(flat_routes[None] == jnp.arange(EXPERTS, dtype=jnp.int32)[:, None, None], flat_mix[None], 0.0), axis=2
    )
    theirs = lax.ppermute(mine, "zl", ((0, 1), (1, 0)))
    mix = jnp.where(zl == 0, jnp.concatenate([mine, theirs], 1), jnp.concatenate([theirs, mine], 1))

    inverse = jnp.zeros((16,), jnp.int32).at[piece_owner].set(jnp.arange(16, dtype=jnp.int32))
    grp = inverse // 2
    source = ((grp % 4 - xi) % 4) * 2 + grp // 4
    tab = jnp.concatenate([jnp.stack([source, inverse % 2], 1).reshape(-1), core.reshape(1)]).astype(jnp.int32)

    moment_new = beta_one * moment_one + (1.0 - beta_one) * gradient
    second_new = beta_two * moment_two + (1.0 - beta_two) * gradient * gradient
    adjust = (
        moment_new / bias_one / (jnp.sqrt(second_new / bias_two) + adam_eps) + decay_rate * master
    )
    updated = (master - learn_rate * adjust).astype(bf16)
    updated = jnp.pad(updated.transpose(0, 2, 1, 3), ((0, 0), (0, 0), (0, ROWS - 45), (0, 3072 - 2880)))

    packed = pl.pallas_call(
        pack_kernel,
        out_shape=jax.ShapeDtypeStruct((32, 5, ROWS, 128), bf16),
        compiler_params=pltpu.CompilerParams(vmem_limit_bytes=32 * 2**20),
        name="pack",
    )(updated)
    w0 = lax.all_to_all(packed, plane, 0, 0)

    up = [(i, (i + 1) % 4) for i in range(4)]
    down = [(i, (i - 1) % 4) for i in range(4)]
    w1a = lax.ppermute(w0[:16], "x", down)
    w3b = lax.ppermute(w0[16:], "x", up)
    w1b = lax.ppermute(w0[16:], "x", down)
    w3a = lax.ppermute(w0[:16], "x", up)
    w2a = lax.ppermute(w1a, "x", down)
    w2b = lax.ppermute(w3b, "x", up)

    own, send = pl.pallas_call(
        expert_kernel,
        out_shape=[jax.ShapeDtypeStruct((16, 192, TOK), bf16)] * 2,
        in_specs=[pl.BlockSpec(memory_space=pltpu.SMEM)] + [pl.BlockSpec(memory_space=pltpu.VMEM)] * 9,
        out_specs=[pl.BlockSpec(memory_space=pltpu.VMEM)] * 2,
        scratch_shapes=[
            pltpu.VMEM((768, 256), bf16),
            pltpu.VMEM((768, 256), bf16),
            pltpu.VMEM((2 * TOK, 256), f32),
            pltpu.VMEM((EXPERTS, 2, 2 * TOK, 256), bf16),
            pltpu.VMEM((768, 2 * TOK), f32),
        ],
        compiler_params=pltpu.CompilerParams(vmem_limit_bytes=56 * 2**20),
        name="experts",
    )(tab, mix, x_all, w0, w1a, w1b, w2a, w2b, w3a, w3b)

    other = lax.ppermute(send, "core", ((0, 1), (1, 0)))
    both = (own.astype(f32) + other.astype(f32)).astype(bf16)
    parts = lax.all_to_all(both, ("zl", "zh", "y"), 0, 0)
    total = jnp.sum(parts.astype(f32), axis=0).astype(bf16)
    total = total.reshape(4, ROWS, TOK)[:, :45].reshape(180, 4, 128)
    return total.transpose(1, 2, 0)


def solution(mesh):
    fine = Mesh(mesh.devices.reshape(2, 4, 2, 4, 2), ("zl", "x", "zh", "y", "core"))
    grp, tp = ("zl", "x"), ("zh", "y", "core")
    state = P(grp, tp, None, None)
    return jax.shard_map(
        shards,
        mesh=fine,
        in_specs=(state, state, state, state, P(), P(None, grp, tp), P(None, grp, None), P(None, grp, None)),
        out_specs=P(None, grp, tp),
        check_vma=False,
    )
```

```python
import functools

import jax
import jax.numpy as jnp
from jax import lax
from jax.experimental import pallas as pl
from jax.experimental.pallas import tpu as pltpu
from jax.sharding import Mesh
from jax.sharding import PartitionSpec as P

EXPERTS = 4
ROWS = 48
PART = 56
TOK = 512
HALF = 1536

learn_rate = 0.003
beta_one = 0.9
beta_two = 0.999
adam_eps = 1e-08
decay_rate = 0.1
bias_one = 1.0 - 0.9**20
bias_two = 1.0 - 0.999**20

bf16 = jnp.bfloat16
f32 = jnp.float32


def roll(x, by):
    if isinstance(by, int):
        by = by % 128
        if by == 0:
            return x
    return pltpu.roll(x, by, 1)


def pack_kernel(place, w_ref, o_ref):
    xl, zl = place[0], place[1]
    lane = lax.broadcasted_iota(jnp.int32, (ROWS, 128), 1)
    lane8 = lax.broadcasted_iota(jnp.int32, (8, 128), 1)
    within = lane % 64

    @pl.loop(0, 8)
    def _(k):
        def tile(s, kind, j):
            return w_ref[s, kind, :, pl.ds(pl.multiple_of(k * 384 + j * 128, 128), 128)].astype(f32)

        for i in range(16):
            a, off = (24 * i) // 128, (24 * i) % 128

            def source(s, kind):
                if off <= 104:
                    return tile(s, kind, a)
                return jnp.where(lane >= off, tile(s, kind, a), tile(s, kind, a + 1))

            pair = 2 * k + i // 8
            link_x, link_z = pair // 4, pair % 4
            jx, jz = (link_x + xl) % 2, (link_z + zl) % 2
            x_to, z_to = (link_x + jx) % 4, (link_z + jz) % 4
            to = (x_to // 2) * 16 + (z_to // 2) * 8 + i % 8
            halves, fold = [], jnp.zeros((8, 128), f32)
            for s in range(2):
                gate, up, down = source(s, 0), source(s, 1), source(s, 2)
                half = 64 * ((s + i // 8) % 2)
                gate, up = roll(gate, half - off), roll(up, half + 24 - off)
                main_down = roll(down, half + 48 - off)
                halves.append(jnp.where(within < 24, gate, jnp.where(within < 48, up, main_down)))
                for g in range(6):
                    at = 16 * g + 8 * s
                    rest = roll(down[8 * g : 8 * g + 8], at - off - 16)
                    fold = jnp.where((lane8 >= at) & (lane8 < at + 8), rest, fold)
            main = jnp.where(lane < 64, halves[i // 8], halves[1 - i // 8])
            o_ref[to, 2 * jx + jz] = jnp.concatenate([main, fold], 0).astype(bf16)


def assemble_kernel(along_x, place, *refs):
    *parts, o_ref = refs
    if len(parts) == 1:
        part = [lambda src, m=m: parts[0][src, m] for m in range(4)]
    elif along_x:
        part = [lambda src, m=m: parts[m // 2][m % 2, src] for m in range(4)]
    else:
        part = [lambda src, m=m: parts[m % 2][m // 2, src] for m in range(4)]
    lane = lax.broadcasted_iota(jnp.int32, (ROWS, 128), 1)
    lane8 = lax.broadcasted_iota(jnp.int32, (8, 128), 1)

    for zl in range(2):

        @pl.when(place[1] == zl)
        def _():
            @pl.loop(0, 32)
            def _(src):
                row = pl.ds(pl.multiple_of((src % 16) * ROWS, ROWS), ROWS)
                loaded = [part[m](src).astype(f32) for m in range(4)]
                for slot in range(2):
                    swap = slot ^ zl
                    for pair in range(2):
                        first, second = loaded[2 * pair], loaded[2 * pair + 1]
                        main = roll(jnp.where((lane // 64) == swap, first[:ROWS], second[:ROWS]), swap * 64)
                        rows = []
                        for g in range(6):
                            at = 16 * g + 8 * slot
                            low, high = roll(second[ROWS:], -at), roll(first[ROWS:], 64 - at)
                            cur = main[8 * g : 8 * g + 8]
                            rows.append(jnp.where(lane8 < 8, low, jnp.where((lane8 // 8) == 8, high, cur)))
                        col = slice(pair * 128, pair * 128 + 128)
                        piece = (src // 16) * 2 + slot
                        o_ref[0, piece, row, col] = main.astype(bf16)
                        o_ref[1, piece, row, col] = jnp.concatenate(rows, 0).astype(bf16)


def expert_kernel(tab, mix_ref, *refs):
    xs, ws, (own_ref, send_ref) = refs[:4], refs[4:8], refs[8:10]
    x, wg, wd, hid, stage, xsem, gsem, dsem, osem = refs[10:]
    core, y = tab[32], tab[33]

    gets = []
    for side in range(2):
        near, rest = xs[2 * side : 2 * side + 2]
        for at in range(4):
            ref = (near, rest)[at // 2].at[pl.ds(at % 2 * 2 * TOK, 2 * TOK)]
            to = x.at[:, pl.ds(side * HALF + at * 384, 384)]
            gets.append(pltpu.make_async_copy(ref, to, xsem.at[len(gets)]))
            gets[-1].start()

    def fetch(use):
        @pl.loop(0, 16)
        def _(i):
            e, b = i // 4, i % 4
            src, slot = tab[2 * i], tab[2 * i + 1]
            piece = (src % 2) * 2 + slot
            for relation in range(4):

                @pl.when(src // 2 == relation)
                def _():
                    for q in range(4):
                        away_y = (2 * (b % 2) + q // 2 + 4 - y) % 4
                        side = (q + core) % 2
                        row = pl.multiple_of(side * HALF + away_y * 384 + (b // 2) * 192, 192)
                        block = ws[relation].at[use, piece, pl.ds(192 * q, 192)]
                        if use == 0:
                            pltpu.make_async_copy(block, wg.at[e, pl.ds(row, 192)], gsem.at[e]).start()
                        else:
                            to = wd.at[pl.ds(row, 192), pl.ds(pl.multiple_of(e * 256, 256), 256)]
                            pltpu.make_async_copy(block, to, dsem).start()

    fetch(0)
    fetch(1)
    for get in gets:
        get.wait()

    lanes = lax.broadcasted_iota(jnp.int32, (2 * TOK, 128), 1) % 64

    @pl.loop(0, EXPERTS)
    def _(e):
        pltpu.make_async_copy(wg.at[e], wg.at[e], gsem.at[e]).wait()
        acc = jnp.dot(x[...], wg[e], preferred_element_type=f32)
        mix = mix_ref[e]
        for n in range(2):
            gate = acc[:, n * 128 : (n + 1) * 128]
            hidden = (pltpu.roll(gate, 104, 1) + 1.0) * gate * jax.nn.sigmoid(1.702 * gate)
            hidden = hidden.astype(bf16).astype(f32) * mix
            hidden = jnp.where((lanes >= 48) | (lanes < 8), pltpu.roll(hidden, 48, 1), 0.0)
            hid[:, pl.ds(pl.multiple_of(e * 256 + n * 128, 128), 128)] = hidden.astype(bf16)

    pltpu.make_async_copy(wd, wd, dsem).wait()

    def put_wait(slot):
        pltpu.make_async_copy(stage.at[slot], stage.at[slot], osem.at[slot]).wait()

    @pl.loop(0, 4)
    def _(k):
        side, n, slot = 1 - k // 2, k % 2, k % 2
        rows = pl.ds(pl.multiple_of(side * HALF + n * 768, 768), 768)
        out = lax.dot_general(wd[rows, :], hid[...], (((1,), (1,)), ((), ())), preferred_element_type=f32)

        @pl.when(k >= 2)
        def _():
            put_wait(slot)

        stage[slot] = out.astype(bf16)
        for ref, want in ((own_ref, 0), (send_ref, 1)):

            @pl.when(side == want)
            def _():
                for q in range(4):
                    for z in range(2):
                        at = 8 * z + 4 * (q % 2) + (2 * n + q // 2 + y) % 4
                        block = stage.at[slot, pl.ds(q * 192, 192), pl.ds(z * TOK, TOK)]
                        pltpu.make_async_copy(block, ref.at[at], osem.at[slot]).start()

    put_wait(0)
    put_wait(1)


def shards(master, moment_one, moment_two, gradient, piece_owner, tokens, routes, mix_weight):
    xl, zl, core = lax.axis_index("xl"), lax.axis_index("zl"), lax.axis_index("core")
    chips = ("xh", "zh", "y")
    swap = ((0, 1), (1, 0))
    plus = [(i, (i + 1) % 4) for i in range(4)]
    minus = [(i, (i - 1) % 4) for i in range(4)]

    own_x = tokens.transpose(2, 0, 1).reshape(4, 45, TOK)
    own_x = jnp.pad(own_x, ((0, 0), (0, ROWS - 45), (0, 0))).reshape(4 * ROWS, TOK)
    xh, zh = lax.axis_index("xh"), lax.axis_index("zh")
    at_z, at_x = lax.ppermute(own_x, "zh", swap), lax.ppermute(own_x, "xh", swap)
    at_xz = lax.ppermute(own_x, ("xh", "zh"), ((0, 3), (1, 2), (2, 1), (3, 0)))

    def in_order(first, here, other):
        return jnp.stack([jnp.where(first, here, other), jnp.where(first, other, here)])

    swapped = own_x, at_z, at_x, at_xz

    flat_routes = routes.reshape(TOK, 2)
    flat_mix = mix_weight.reshape(TOK, 2)
    mine = jnp.sum(
        jnp.where(flat_routes[None] == jnp.arange(EXPERTS, dtype=jnp.int32)[:, None, None], flat_mix[None], 0.0), axis=2
    )
    theirs = lax.ppermute(mine, "xh", swap)
    mix = jnp.where(
        xh == 0, jnp.concatenate([mine, theirs], 1), jnp.concatenate([theirs, mine], 1)
    )

    inverse = jnp.zeros((16,), jnp.int32).at[piece_owner].set(jnp.arange(16, dtype=jnp.int32))
    grp = inverse // 2
    relation = ((grp % 2) ^ xl) * 2 + ((grp // 4) ^ zl)
    source = relation * 2 + (grp % 4) // 2
    tab = jnp.concatenate([jnp.stack([source, inverse % 2], 1).reshape(-1), jnp.stack([core, lax.axis_index("y")])]).astype(jnp.int32)
    place = jnp.stack([xl, zl]).astype(jnp.int32)

    moment_new = beta_one * moment_one + (1.0 - beta_one) * gradient
    second_new = beta_two * moment_two + (1.0 - beta_two) * gradient * gradient
    adjust = (
        moment_new / bias_one / (jnp.sqrt(second_new / bias_two) + adam_eps) + decay_rate * master
    )
    updated = (master - learn_rate * adjust).astype(bf16)
    updated = jnp.pad(updated.transpose(0, 2, 1, 3), ((0, 0), (0, 0), (0, ROWS - 45), (0, 3072 - 2880)))

    smem, vmem = pl.BlockSpec(memory_space=pltpu.SMEM), pl.BlockSpec(memory_space=pltpu.VMEM)
    packed = pl.pallas_call(
        pack_kernel,
        out_shape=jax.ShapeDtypeStruct((32, 4, PART, 128), bf16),
        in_specs=[smem, vmem],
        out_specs=vmem,
        compiler_params=pltpu.CompilerParams(vmem_limit_bytes=32 * 2**20),
        name="pack",
    )(place, updated)
    packed, swapped, mix = lax.optimization_barrier((packed, swapped, mix))
    w0 = lax.all_to_all(packed, ("xh", "zh", "y", "core"), 0, 0)
    held = in_order(xh == 0, in_order(zh == 0, *swapped[:2]), in_order(zh == 0, *swapped[2:]))
    held = held.transpose(0, 3, 1, 2).reshape(2 * TOK, 384)
    held, w0 = lax.optimization_barrier((held, w0))

    ax, az = ("xh", "xl"), ("zl", "zh")
    plus_z = [((i % 2) * 2 + i // 2, (j % 2) * 2 + j // 2) for i, j in plus]
    minus_z = [(j, i) for i, j in plus_z]

    def along_x(block, i):
        return lax.ppermute(block, ax, plus if i else minus)

    def along_z(block, j):
        return lax.ppermute(block, az, plus_z if j else minus_z)

    grid = w0.reshape(32, 2, 2, PART, 128)
    from_x = [along_x(jnp.swapaxes(grid[:, 1 - i], 0, 1), i) for i in range(2)]
    from_z = [along_z(jnp.swapaxes(grid[:, :, 1 - j], 0, 1), j) for j in range(2)]

    def assemble(parts, name):
        return pl.pallas_call(
            functools.partial(assemble_kernel, name != "pieces_z"),
            out_shape=jax.ShapeDtypeStruct((2, 4, 768, 256), bf16),
            in_specs=[smem] + [vmem] * len(parts),
            out_specs=vmem,
            compiler_params=pltpu.CompilerParams(vmem_limit_bytes=32 * 2**20),
            cost_estimate=pl.CostEstimate(flops=0, bytes_accessed=16 * 2**20, transcendentals=0),
            name=name,
        )(place, *parts)

    above = lax.ppermute(held, "y", minus)
    mix = jnp.broadcast_to(mix[:, :, None], (EXPERTS, 2 * TOK, 128))
    place, mix = lax.optimization_barrier((place, mix))
    here = assemble([w0], "pieces_here")
    above, from_x, from_z, here = lax.optimization_barrier((above, from_x, from_z, here))

    diagonal = [along_x(jnp.stack([from_z[0][1 - i], from_z[1][1 - i]]), i) for i in range(2)]
    below, far = lax.ppermute(held, "y", plus), lax.ppermute(above, "y", minus)
    near = jnp.concatenate([held, above], 0)
    x_near = lax.ppermute(near, "core", swap)
    ws = [here, assemble(from_z, "pieces_z"), assemble(from_x, "pieces_x")]
    diagonal, below, far, x_near, ws = lax.optimization_barrier((diagonal, below, far, x_near, ws))
    rest = jnp.concatenate([far, below], 0)
    x_rest = lax.ppermute(rest, "core", swap)
    ws.append(assemble(diagonal, "pieces_diagonal"))
    xs = [near, rest, x_near, x_rest]

    hbm = pl.BlockSpec(memory_space=pl.ANY)
    own_sum, send = pl.pallas_call(
        expert_kernel,
        out_shape=[jax.ShapeDtypeStruct((16, 192, TOK), bf16)] * 2,
        in_specs=[smem, vmem] + [hbm] * 8,
        out_specs=[hbm] * 2,
        scratch_shapes=[
            pltpu.VMEM((2 * TOK, 2 * HALF), bf16),
            pltpu.VMEM((EXPERTS, 2 * HALF, 256), bf16),
            pltpu.VMEM((2 * HALF, EXPERTS * 256), bf16),
            pltpu.VMEM((2 * TOK, EXPERTS * 256), bf16),
            pltpu.VMEM((2, 768, 2 * TOK), bf16),
            pltpu.SemaphoreType.DMA((8,)),
            pltpu.SemaphoreType.DMA((EXPERTS,)),
            pltpu.SemaphoreType.DMA,
            pltpu.SemaphoreType.DMA((2,)),
        ],
        compiler_params=pltpu.CompilerParams(vmem_limit_bytes=58 * 2**20),
        name="experts",
    )(tab, mix, *xs, *ws)

    other = lax.ppermute(send, "core", swap)
    both = (own_sum.astype(f32) + other.astype(f32)).astype(bf16)
    parts = lax.all_to_all(both, chips, 0, 0)
    total = jnp.sum(parts.astype(f32), axis=0).astype(bf16)
    total = total.reshape(4, ROWS, TOK)[:, :45].reshape(180, 4, 128)
    return total.transpose(1, 2, 0)


def solution(mesh):
    fine = Mesh(mesh.devices.reshape(2, 2, 2, 2, 4, 2), ("zl", "xh", "xl", "zh", "y", "core"))
    grp, tp = ("zl", "xh", "xl"), ("zh", "y", "core")
    state = P(grp, tp, None, None)
    return jax.shard_map(
        shards,
        mesh=fine,
        in_specs=(state, state, state, state, P(), P(None, grp, tp), P(None, grp, None), P(None, grp, None)),
        out_specs=P(None, grp, tp),
        check_vma=False,
    )
```

```python
import functools

import jax
import jax.numpy as jnp
from jax import lax
from jax.experimental import pallas as pl
from jax.experimental.pallas import tpu as pltpu
from jax.sharding import Mesh
from jax.sharding import PartitionSpec as P

EXPERTS = 4
ROWS = 48
PART = 56
TOK = 512
HALF = 1536

learn_rate = 0.003
beta_one = 0.9
beta_two = 0.999
adam_eps = 1e-08
decay_rate = 0.1
bias_one = 1.0 - 0.9**20
bias_two = 1.0 - 0.999**20

bf16 = jnp.bfloat16
f32 = jnp.float32


def roll(x, by):
    if isinstance(by, int):
        by = by % 128
        if by == 0:
            return x
    return pltpu.roll(x, by, 1)


def pack_kernel(place, w_ref, o_ref):
    xl, zl = place[0], place[1]
    lane = lax.broadcasted_iota(jnp.int32, (ROWS, 128), 1)
    lane8 = lax.broadcasted_iota(jnp.int32, (8, 128), 1)
    within = lane % 64

    @pl.loop(0, 8)
    def _(k):
        def tile(s, kind, j):
            return w_ref[s, kind, :, pl.ds(pl.multiple_of(k * 384 + j * 128, 128), 128)].astype(f32)

        for i in range(16):
            a, off = (24 * i) // 128, (24 * i) % 128

            def source(s, kind):
                if off <= 104:
                    return tile(s, kind, a)
                return jnp.where(lane >= off, tile(s, kind, a), tile(s, kind, a + 1))

            pair = 2 * k + i // 8
            link_x, link_z = pair // 4, pair % 4
            jx, jz = (link_x + xl) % 2, (link_z + zl) % 2
            x_to, z_to = (link_x + jx) % 4, (link_z + jz) % 4
            to = (x_to // 2) * 16 + (z_to // 2) * 8 + i % 8
            halves, fold = [], jnp.zeros((8, 128), f32)
            for s in range(2):
                gate, up, down = source(s, 0), source(s, 1), source(s, 2)
                half = 64 * ((s + i // 8) % 2)
                gate, up = roll(gate, half - off), roll(up, half + 24 - off)
                main_down = roll(down, half + 48 - off)
                halves.append(jnp.where(within < 24, gate, jnp.where(within < 48, up, main_down)))
                for g in range(6):
                    at = 16 * g + 8 * s
                    rest = roll(down[8 * g : 8 * g + 8], at - off - 16)
                    fold = jnp.where((lane8 >= at) & (lane8 < at + 8), rest, fold)
            main = jnp.where(lane < 64, halves[i // 8], halves[1 - i // 8])
            o_ref[to, 2 * jx + jz] = jnp.concatenate([main, fold], 0).astype(bf16)


def assemble_kernel(along_x, place, *refs):
    *parts, o_ref = refs
    if len(parts) == 1:
        part = [lambda src, m=m: parts[0][src, m] for m in range(4)]
    elif along_x:
        part = [lambda src, m=m: parts[m // 2][m % 2, src] for m in range(4)]
    else:
        part = [lambda src, m=m: parts[m % 2][m // 2, src] for m in range(4)]
    lane = lax.broadcasted_iota(jnp.int32, (ROWS, 128), 1)
    lane8 = lax.broadcasted_iota(jnp.int32, (8, 128), 1)

    for zl in range(2):

        @pl.when(place[1] == zl)
        def _():
            @pl.loop(0, 32)
            def _(src):
                chunk = src % 16
                side = (chunk // 4 + place[2]) % 2
                row = (2 * side + chunk // 8) * 192 + (chunk % 4) * ROWS
                row = pl.ds(pl.multiple_of(row, ROWS), ROWS)
                loaded = [part[m](src).astype(f32) for m in range(4)]
                for slot in range(2):
                    swap = slot ^ zl
                    for pair in range(2):
                        first, second = loaded[2 * pair], loaded[2 * pair + 1]
                        main = roll(jnp.where((lane // 64) == swap, first[:ROWS], second[:ROWS]), swap * 64)
                        rows = []
                        for g in range(6):
                            at = 16 * g + 8 * slot
                            low, high = roll(second[ROWS:], -at), roll(first[ROWS:], 64 - at)
                            cur = main[8 * g : 8 * g + 8]
                            rows.append(jnp.where(lane8 < 8, low, jnp.where((lane8 // 8) == 8, high, cur)))
                        col = slice(pair * 128, pair * 128 + 128)
                        piece = (src // 16) * 2 + slot
                        o_ref[0, piece, row, col] = main.astype(bf16)
                        o_ref[1, piece, row, col] = jnp.concatenate(rows, 0).astype(bf16)


def fetch_pieces(tab, ws, use, experts, start):
    @pl.loop(4 * experts[0], 4 * experts[1])
    def _(i):
        src, slot = tab[2 * i], tab[2 * i + 1]
        for relation in range(4):

            @pl.when(src // 2 == relation)
            def _():
                start(i // 4, i % 4, ws[relation].at[use, (src % 2) * 2 + slot])


def wait_all(ref, sem):
    pltpu.make_async_copy(ref, ref, sem).wait()


def fetch_down(tab, ws, wd, dsem, side):
    def start(e, b, block):
        to = wd.at[pl.ds(2 * (b % 2), 2), b // 2, :, pl.ds(pl.multiple_of(e * 256, 256), 256)]
        pltpu.make_async_copy(block.at[side], to, dsem).start()

    fetch_pieces(tab, ws, 1, (0, EXPERTS), start)


def down(wd, hid, stage, osem, out_ref):
    for n in range(2):
        rows = wd[2 * n : 2 * n + 2].reshape(768, EXPERTS * 256)
        out = lax.dot_general(rows, hid[...], (((1,), (1,)), ((), ())), preferred_element_type=f32)
        stage[n] = out.astype(bf16)
        for q in range(4):
            for z in range(2):
                at = 8 * z + 4 * (q % 2) + 2 * n + q // 2
                block = stage.at[n, pl.ds(q * 192, 192), pl.ds(z * TOK, TOK)]
                pltpu.make_async_copy(block, out_ref.at[at], osem.at[n]).start()
    for n in range(2):
        wait_all(stage.at[n], osem.at[n])


def hidden_kernel(tab, *refs):
    xs, ws, mix_ref, (send_ref, hid, wd_own) = refs[:8], refs[8:12], refs[12], refs[13:16]
    x, wg, wd, stage, mix, xsem, gsem, dsem, osem, msem = refs[16:]
    y = tab[32]

    def start(e, b, block):
        to = wg.at[e, :, pl.ds(2 * (b % 2), 2), b // 2]
        pltpu.make_async_copy(block, to, gsem.at[e]).start()

    gets = []
    for side in range(2):
        for n, ref in enumerate(xs[4 * side : 4 * side + 4]):
            lanes = pl.ds(pl.multiple_of(side * HALF + ((y + n) % 4) * 384, 128), 384)
            gets.append(pltpu.make_async_copy(ref, x.at[:, lanes], xsem.at[len(gets)]))
            gets[-1].start()
    fetch_pieces(tab, ws, 0, (0, EXPERTS), start)
    gets.append(pltpu.make_async_copy(mix_ref, mix, msem))
    gets[-1].start()
    fetch_down(tab, ws, wd, dsem.at[1], 1)
    fetch_down(tab, ws, wd_own, dsem.at[0], 0)
    for get in gets:
        get.wait()

    lanes = lax.broadcasted_iota(jnp.int32, (2 * TOK, 128), 1) % 64

    @pl.loop(0, EXPERTS)
    def _(e):
        wait_all(wg.at[e], gsem.at[e])
        acc = jnp.dot(x[...], wg[e].reshape(2 * HALF, 256), preferred_element_type=f32)
        for n in range(2):
            gate = acc[:, n * 128 : (n + 1) * 128]
            hidden = (pltpu.roll(gate, 104, 1) + 1.0) * gate * jax.nn.sigmoid(1.702 * gate)
            hidden = hidden.astype(bf16).astype(f32) * mix[e]
            hidden = jnp.where((lanes >= 48) | (lanes < 8), pltpu.roll(hidden, 48, 1), 0.0)
            hid[:, pl.ds(pl.multiple_of(e * 256 + n * 128, 128), 128)] = hidden.astype(bf16)

    wait_all(wd, dsem.at[1])
    down(wd, hid, stage, osem, send_ref)
    wait_all(wd_own, dsem.at[0])


def own_kernel(wd, hid, own_ref, stage, osem):
    down(wd, hid, stage, osem, own_ref)


def update(master, moment_one, moment_two, gradient):
    moment_new = beta_one * moment_one + (1.0 - beta_one) * gradient
    second_new = beta_two * moment_two + (1.0 - beta_two) * gradient * gradient
    adjust = (
        moment_new / bias_one / (jnp.sqrt(second_new / bias_two) + adam_eps) + decay_rate * master
    )
    updated = (master - learn_rate * adjust).astype(bf16)
    return jnp.pad(updated.transpose(0, 2, 1, 3), ((0, 0), (0, 0), (0, ROWS - 45), (0, 3072 - 2880)))


def shards(master, moment_one, moment_two, gradient, piece_owner, tokens, routes, mix_weight):
    xl, zl, core = lax.axis_index("xl"), lax.axis_index("zl"), lax.axis_index("core")
    chips = ("xh", "zh", "y")
    swap = ((0, 1), (1, 0))
    plus = [(i, (i + 1) % 4) for i in range(4)]
    minus = [(i, (i - 1) % 4) for i in range(4)]

    own_x = tokens.transpose(2, 0, 1).reshape(4, 45, TOK)
    own_x = jnp.pad(own_x, ((0, 0), (0, ROWS - 45), (0, 0))).reshape(4 * ROWS, TOK)
    xh, zh = lax.axis_index("xh"), lax.axis_index("zh")
    at_z, at_x = lax.ppermute(own_x, "zh", swap), lax.ppermute(own_x, "xh", swap)
    def in_order(first, here, other):
        return jnp.stack([jnp.where(first, here, other), jnp.where(first, other, here)])


    flat_routes = routes.reshape(TOK, 2)
    flat_mix = mix_weight.reshape(TOK, 2)
    mine = jnp.sum(
        jnp.where(flat_routes[None] == jnp.arange(EXPERTS, dtype=jnp.int32)[:, None, None], flat_mix[None], 0.0), axis=2
    )
    updated = update(master, moment_one, moment_two, gradient)
    updated, at_x, mine = lax.optimization_barrier((updated, at_x, mine))
    swapped = own_x, at_z, at_x, lax.ppermute(at_x, "zh", swap)
    theirs = lax.ppermute(mine, "xh", swap)

    inverse = jnp.zeros((16,), jnp.int32).at[piece_owner].set(jnp.arange(16, dtype=jnp.int32))
    grp = inverse // 2
    relation = ((grp % 2) ^ xl) * 2 + ((grp // 4) ^ zl)
    source = relation * 2 + (grp % 4) // 2
    tab = jnp.concatenate([jnp.stack([source, inverse % 2], 1).reshape(-1), lax.axis_index("y").reshape(1)]).astype(jnp.int32)
    place = jnp.stack([xl, zl, core]).astype(jnp.int32)

    smem, vmem = pl.BlockSpec(memory_space=pltpu.SMEM), pl.BlockSpec(memory_space=pltpu.VMEM)
    packed = pl.pallas_call(
        pack_kernel,
        out_shape=jax.ShapeDtypeStruct((32, 4, PART, 128), bf16),
        in_specs=[smem, vmem],
        out_specs=vmem,
        compiler_params=pltpu.CompilerParams(vmem_limit_bytes=16 * 2**20),
        name="pack",
    )(place, updated)
    packed, swapped, theirs = lax.optimization_barrier((packed, swapped, theirs))
    w0 = lax.all_to_all(packed, ("xh", "zh", "y", "core"), 0, 0)
    held = in_order(xh == 0, in_order(zh == 0, *swapped[:2]), in_order(zh == 0, *swapped[2:]))
    held = held.transpose(0, 3, 1, 2).reshape(2 * TOK, 384)

    ax, az = ("xh", "xl"), ("zl", "zh")
    plus_z = [((i % 2) * 2 + i // 2, (j % 2) * 2 + j // 2) for i, j in plus]
    minus_z = [(j, i) for i, j in plus_z]

    def along_x(block, i):
        return lax.ppermute(block, ax, plus if i else minus)

    def along_z(block, j):
        return lax.ppermute(block, az, plus_z if j else minus_z)

    grid = w0.reshape(32, 2, 2, PART, 128)
    from_x = [along_x(jnp.swapaxes(grid[:, 1 - i], 0, 1), i) for i in range(2)]
    from_z = [along_z(jnp.swapaxes(grid[:, :, 1 - j], 0, 1), j) for j in range(2)]

    def assemble(parts, name):
        return pl.pallas_call(
            functools.partial(assemble_kernel, name != "pieces_z"),
            out_shape=jax.ShapeDtypeStruct((2, 4, 768, 256), bf16),
            in_specs=[smem] + [vmem] * len(parts),
            out_specs=vmem,
            compiler_params=pltpu.CompilerParams(vmem_limit_bytes=16 * 2**20),
            cost_estimate=pl.CostEstimate(flops=0, bytes_accessed=16 * 2**20, transcendentals=0),
            name=name,
        )(place, *parts).reshape(2, 4, 2, 2, 192, 256)

    x_held = lax.ppermute(held, "core", swap)
    held, x_held = lax.optimization_barrier((held, x_held))
    above = lax.ppermute(held, "y", minus)
    mix = jnp.where(
        xh == 0, jnp.concatenate([mine, theirs], 1), jnp.concatenate([theirs, mine], 1)
    )
    mix = jnp.broadcast_to(mix[:, :, None], (EXPERTS, 2 * TOK, 128))
    place, mix, tab = lax.optimization_barrier((place, mix, tab))
    here = assemble([w0], "pieces_here")
    above, from_x, from_z, here = lax.optimization_barrier((above, from_x, from_z, here))

    diagonal = [along_x(jnp.stack([from_z[0][1 - i], from_z[1][1 - i]]), i) for i in range(2)]
    below, far = lax.ppermute(held, "y", plus), lax.ppermute(above, "y", minus)
    x_above = lax.ppermute(above, "core", swap)
    ws = [here, assemble(from_z, "pieces_z"), assemble(from_x, "pieces_x")]
    diagonal, below, far, x_above, ws = lax.optimization_barrier((diagonal, below, far, x_above, ws))
    x_below, x_far = lax.ppermute(below, "core", swap), lax.ppermute(far, "core", swap)
    ws.append(assemble(diagonal, "pieces_diagonal"))
    xs = [held, above, far, below, x_held, x_above, x_far, x_below]

    hbm, anywhere = pl.BlockSpec(memory_space=pltpu.HBM), pl.BlockSpec(memory_space=pl.ANY)
    sums = jax.ShapeDtypeStruct((16, 192, TOK), bf16)
    hidden = jax.ShapeDtypeStruct((2 * TOK, EXPERTS * 256), bf16)
    down_half = jax.ShapeDtypeStruct((4, 2, 192, EXPERTS * 256), bf16)
    dma = pltpu.SemaphoreType.DMA
    stage = pltpu.VMEM((2, 768, 2 * TOK), bf16)
    send, hidden, down_own = pl.pallas_call(
        hidden_kernel,
        out_shape=[sums, hidden, down_half],
        in_specs=[smem] + [hbm] * 13,
        out_specs=[hbm, vmem, vmem],
        scratch_shapes=[
            pltpu.VMEM((2 * TOK, 2 * HALF), bf16),
            pltpu.VMEM((EXPERTS, 2, 4, 2, 192, 256), bf16),
            pltpu.VMEM(down_half.shape, bf16),
            stage,
            pltpu.VMEM((EXPERTS, 2 * TOK, 128), f32),
            dma((8,)),
            dma((EXPERTS,)),
            dma((2,)),
            dma((2,)),
            dma,
        ],
        compiler_params=pltpu.CompilerParams(vmem_limit_bytes=40 * 2**20),
        name="hidden",
    )(tab, *xs, *ws, mix)
    other = lax.ppermute(send, "core", swap)
    own_sum = pl.pallas_call(
        own_kernel,
        out_shape=sums,
        in_specs=[vmem] * 2,
        out_specs=anywhere,
        scratch_shapes=[stage, dma((2,))],
        compiler_params=pltpu.CompilerParams(vmem_limit_bytes=24 * 2**20),
        cost_estimate=pl.CostEstimate(flops=2 * HALF * 2 * TOK * 1024, bytes_accessed=8 * 2**20, transcendentals=0),
        name="own_side",
    )(down_own, hidden)
    both = (own_sum.astype(f32) + other.astype(f32)).astype(bf16)
    parts = lax.all_to_all(both, chips, 0, 0)
    total = jnp.sum(parts.astype(f32), axis=0).astype(bf16)
    total = total.reshape(4, ROWS, TOK)[:, :45].reshape(180, 4, 128)
    return total.transpose(1, 2, 0)


def solution(mesh):
    fine = Mesh(mesh.devices.reshape(2, 2, 2, 2, 4, 2), ("zl", "xh", "xl", "zh", "y", "core"))
    grp, tp = ("zl", "xh", "xl"), ("zh", "y", "core")
    state = P(grp, tp, None, None)
    return jax.shard_map(
        shards,
        mesh=fine,
        in_specs=(state, state, state, state, P(), P(None, grp, tp), P(None, grp, None), P(None, grp, None)),
        out_specs=P(None, grp, tp),
        check_vma=False,
    )
```

```python
import functools

import jax
import jax.numpy as jnp
from jax import lax
from jax.experimental import pallas as pl
from jax.experimental.pallas import tpu as pltpu
from jax.sharding import Mesh
from jax.sharding import PartitionSpec as P

EXPERTS = 4
ROWS = 48
PART = 56
TOK = 512
HALF = 1536

learn_rate = 0.003
beta_one = 0.9
beta_two = 0.999
adam_eps = 1e-08
decay_rate = 0.1
bias_one = 1.0 - 0.9**20
bias_two = 1.0 - 0.999**20

bf16 = jnp.bfloat16
f32 = jnp.float32


def roll(x, by):
    if isinstance(by, int):
        by = by % 128
        if by == 0:
            return x
    return pltpu.roll(x, by, 1)


def pack_kernel(place, w_ref, o_ref):
    xl, zl = place[0], place[1]
    lane = lax.broadcasted_iota(jnp.int32, (ROWS, 128), 1)
    lane8 = lax.broadcasted_iota(jnp.int32, (8, 128), 1)
    within = lane % 64

    @pl.loop(0, 8)
    def _(k):
        def tile(s, kind, j):
            return w_ref[s, kind, :, pl.ds(pl.multiple_of(k * 384 + j * 128, 128), 128)].astype(f32)

        for i in range(16):
            a, off = (24 * i) // 128, (24 * i) % 128

            def source(s, kind):
                if off <= 104:
                    return tile(s, kind, a)
                return jnp.where(lane >= off, tile(s, kind, a), tile(s, kind, a + 1))

            pair = 2 * k + i // 8
            link_x, link_z = pair // 4, pair % 4
            jx, jz = (link_x + xl) % 2, (link_z + zl) % 2
            x_to, z_to = (link_x + jx) % 4, (link_z + jz) % 4
            to = (x_to // 2) * 16 + (z_to // 2) * 8 + i % 8
            halves, fold = [], jnp.zeros((8, 128), f32)
            for s in range(2):
                gate, up, down = source(s, 0), source(s, 1), source(s, 2)
                half = 64 * ((s + i // 8) % 2)
                gate, up = roll(gate, half - off), roll(up, half + 24 - off)
                main_down = roll(down, half + 48 - off)
                halves.append(jnp.where(within < 24, gate, jnp.where(within < 48, up, main_down)))
                for g in range(6):
                    at = 16 * g + 8 * s
                    rest = roll(down[8 * g : 8 * g + 8], at - off - 16)
                    fold = jnp.where((lane8 >= at) & (lane8 < at + 8), rest, fold)
            main = jnp.where(lane < 64, halves[i // 8], halves[1 - i // 8])
            o_ref[to, 2 * jx + jz] = jnp.concatenate([main, fold], 0).astype(bf16)


def assemble_kernel(along_x, place, *refs):
    *parts, o_ref = refs
    if len(parts) == 1:
        part = [lambda src, m=m: parts[0][src, m] for m in range(4)]
    elif along_x:
        part = [lambda src, m=m: parts[m // 2][m % 2, src] for m in range(4)]
    else:
        part = [lambda src, m=m: parts[m % 2][m // 2, src] for m in range(4)]
    lane = lax.broadcasted_iota(jnp.int32, (ROWS, 128), 1)
    lane8 = lax.broadcasted_iota(jnp.int32, (8, 128), 1)

    for zl in range(2):

        @pl.when(place[1] == zl)
        def _():
            @pl.loop(0, 32)
            def _(src):
                chunk = src % 16
                side = (chunk // 4 + place[2]) % 2
                row = (2 * side + chunk // 8) * 192 + (chunk % 4) * ROWS
                row = pl.ds(pl.multiple_of(row, ROWS), ROWS)
                loaded = [part[m](src).astype(f32) for m in range(4)]
                for slot in range(2):
                    swap = slot ^ zl
                    for pair in range(2):
                        first, second = loaded[2 * pair], loaded[2 * pair + 1]
                        main = roll(jnp.where((lane // 64) == swap, first[:ROWS], second[:ROWS]), swap * 64)
                        rows = []
                        for g in range(6):
                            at = 16 * g + 8 * slot
                            low, high = roll(second[ROWS:], -at), roll(first[ROWS:], 64 - at)
                            cur = main[8 * g : 8 * g + 8]
                            rows.append(jnp.where(lane8 < 8, low, jnp.where((lane8 // 8) == 8, high, cur)))
                        col = slice(pair * 128, pair * 128 + 128)
                        piece = (src // 16) * 2 + slot
                        o_ref[0, piece, row, col] = main.astype(bf16)
                        o_ref[1, piece, row, col] = jnp.concatenate(rows, 0).astype(bf16)


def fetch_pieces(tab, ws, use, experts, start):
    @pl.loop(4 * experts[0], 4 * experts[1])
    def _(i):
        src, slot = tab[2 * i], tab[2 * i + 1]
        for relation in range(4):

            @pl.when(src // 2 == relation)
            def _():
                start(i // 4, i % 4, ws[relation].at[use, (src % 2) * 2 + slot])


def wait_all(ref, sem):
    pltpu.make_async_copy(ref, ref, sem).wait()


def fetch_down(tab, ws, wd, dsem, side):
    def start(e, b, block):
        to = wd.at[pl.ds(2 * (b % 2), 2), b // 2, :, pl.ds(pl.multiple_of(e * 256, 256), 256)]
        pltpu.make_async_copy(block.at[side], to, dsem).start()

    fetch_pieces(tab, ws, 1, (0, EXPERTS), start)


def down(wd, hid, stage, osem, out_ref):
    for n in range(2):
        rows = wd[2 * n : 2 * n + 2].reshape(768, EXPERTS * 256)
        out = lax.dot_general(rows, hid[...], (((1,), (1,)), ((), ())), preferred_element_type=f32)
        stage[n] = out.astype(bf16)
        for q in range(4):
            for z in range(2):
                at = 8 * z + 4 * (q % 2) + 2 * n + q // 2
                block = stage.at[n, pl.ds(q * 192, 192), pl.ds(z * TOK, TOK)]
                pltpu.make_async_copy(block, out_ref.at[at], osem.at[n]).start()
    for n in range(2):
        wait_all(stage.at[n], osem.at[n])


def hidden_kernel(tab, *refs):
    xs, ws, mix_ref, (send_ref, hid, wd_own) = refs[:8], refs[8:12], refs[12], refs[13:16]
    x, wg, wd, stage, mix, xsem, gsem, dsem, osem, msem = refs[16:]
    y = tab[32]

    def start(e, b, block):
        to = wg.at[e, :, pl.ds(2 * (b % 2), 2), b // 2]
        pltpu.make_async_copy(block, to, gsem.at[e]).start()

    gets = []
    for side in range(2):
        for n, ref in enumerate(xs[4 * side : 4 * side + 4]):
            lanes = pl.ds(pl.multiple_of(side * HALF + ((y + n) % 4) * 384, 128), 384)
            gets.append(pltpu.make_async_copy(ref, x.at[:, lanes], xsem.at[len(gets)]))
            gets[-1].start()
    fetch_pieces(tab, ws, 0, (0, EXPERTS), start)
    gets.append(pltpu.make_async_copy(mix_ref, mix, msem))
    gets[-1].start()
    fetch_down(tab, ws, wd, dsem.at[1], 1)
    fetch_down(tab, ws, wd_own, dsem.at[0], 0)
    for get in gets:
        get.wait()

    lanes = lax.broadcasted_iota(jnp.int32, (2 * TOK, 128), 1) % 64

    @pl.loop(0, EXPERTS)
    def _(e):
        wait_all(wg.at[e], gsem.at[e])
        acc = jnp.dot(x[...], wg[e].reshape(2 * HALF, 256), preferred_element_type=f32)
        for n in range(2):
            gate = acc[:, n * 128 : (n + 1) * 128]
            hidden = (pltpu.roll(gate, 104, 1) + 1.0) * gate * jax.nn.sigmoid(1.702 * gate)
            hidden = hidden.astype(bf16).astype(f32) * mix[e]
            hidden = jnp.where((lanes >= 48) | (lanes < 8), pltpu.roll(hidden, 48, 1), 0.0)
            hid[:, pl.ds(pl.multiple_of(e * 256 + n * 128, 128), 128)] = hidden.astype(bf16)

    wait_all(wd, dsem.at[1])
    down(wd, hid, stage, osem, send_ref)
    wait_all(wd_own, dsem.at[0])


def own_kernel(wd, hid, own_ref, stage, osem):
    down(wd, hid, stage, osem, own_ref)


def update(master, moment_one, moment_two, gradient):
    moment_new = beta_one * moment_one + (1.0 - beta_one) * gradient
    second_new = beta_two * moment_two + (1.0 - beta_two) * gradient * gradient
    adjust = (
        moment_new / bias_one / (jnp.sqrt(second_new / bias_two) + adam_eps) + decay_rate * master
    )
    updated = (master - learn_rate * adjust).astype(bf16)
    return jnp.pad(updated.transpose(0, 2, 1, 3), ((0, 0), (0, 0), (0, ROWS - 45), (0, 3072 - 2880)))


def shards(master, moment_one, moment_two, gradient, piece_owner, tokens, routes, mix_weight):
    xl, zl, core = lax.axis_index("xl"), lax.axis_index("zl"), lax.axis_index("core")
    chips = ("xh", "zh", "y")
    swap = ((0, 1), (1, 0))
    plus = [(i, (i + 1) % 4) for i in range(4)]
    minus = [(i, (i - 1) % 4) for i in range(4)]

    own_x = tokens.transpose(2, 0, 1).reshape(4, 45, TOK)
    own_x = jnp.pad(own_x, ((0, 0), (0, ROWS - 45), (0, 0))).reshape(4 * ROWS, TOK)
    xh, zh = lax.axis_index("xh"), lax.axis_index("zh")
    at_z, at_x = lax.ppermute(own_x, "zh", swap), lax.ppermute(own_x, "xh", swap)
    def in_order(first, here, other):
        return jnp.stack([jnp.where(first, here, other), jnp.where(first, other, here)])


    flat_routes = routes.reshape(TOK, 2)
    flat_mix = mix_weight.reshape(TOK, 2)
    mine = jnp.sum(
        jnp.where(flat_routes[None] == jnp.arange(EXPERTS, dtype=jnp.int32)[:, None, None], flat_mix[None], 0.0), axis=2
    )
    updated = update(master, moment_one, moment_two, gradient)
    updated, at_x, mine = lax.optimization_barrier((updated, at_x, mine))
    swapped = own_x, at_z, at_x, lax.ppermute(at_x, "zh", swap)
    theirs = lax.ppermute(mine, "xh", swap)

    inverse = jnp.zeros((16,), jnp.int32).at[piece_owner].set(jnp.arange(16, dtype=jnp.int32))
    grp = inverse // 2
    relation = ((grp % 2) ^ xl) * 2 + ((grp // 4) ^ zl)
    source = relation * 2 + (grp % 4) // 2
    tab = jnp.concatenate([jnp.stack([source, inverse % 2], 1).reshape(-1), lax.axis_index("y").reshape(1)]).astype(jnp.int32)
    place = jnp.stack([xl, zl, core]).astype(jnp.int32)

    smem, vmem = pl.BlockSpec(memory_space=pltpu.SMEM), pl.BlockSpec(memory_space=pltpu.VMEM)
    packed = pl.pallas_call(
        pack_kernel,
        out_shape=jax.ShapeDtypeStruct((32, 4, PART, 128), bf16),
        in_specs=[smem, vmem],
        out_specs=vmem,
        compiler_params=pltpu.CompilerParams(vmem_limit_bytes=16 * 2**20),
        name="pack",
    )(place, updated)
    packed, swapped, theirs = lax.optimization_barrier((packed, swapped, theirs))
    w0 = lax.all_to_all(packed, ("xh", "zh", "y", "core"), 0, 0)
    held = in_order(xh == 0, in_order(zh == 0, *swapped[:2]), in_order(zh == 0, *swapped[2:]))
    held = held.transpose(0, 3, 1, 2).reshape(2 * TOK, 384)

    ax, az = ("xh", "xl"), ("zl", "zh")
    plus_z = [((i % 2) * 2 + i // 2, (j % 2) * 2 + j // 2) for i, j in plus]
    minus_z = [(j, i) for i, j in plus_z]

    def along_x(block, i):
        return lax.ppermute(block, ax, plus if i else minus)

    def along_z(block, j):
        return lax.ppermute(block, az, plus_z if j else minus_z)

    grid = w0.reshape(32, 2, 2, PART, 128)
    from_x = [along_x(jnp.swapaxes(grid[:, 1 - i], 0, 1), i) for i in range(2)]
    from_z = [along_z(jnp.swapaxes(grid[:, :, 1 - j], 0, 1), j) for j in range(2)]

    def assemble(parts, name):
        return pl.pallas_call(
            functools.partial(assemble_kernel, name != "pieces_z"),
            out_shape=jax.ShapeDtypeStruct((2, 4, 768, 256), bf16),
            in_specs=[smem] + [vmem] * len(parts),
            out_specs=vmem,
            compiler_params=pltpu.CompilerParams(vmem_limit_bytes=16 * 2**20),
            cost_estimate=pl.CostEstimate(flops=0, bytes_accessed=16 * 2**20, transcendentals=0),
            name=name,
        )(place, *parts).reshape(2, 4, 2, 2, 192, 256)

    x_held = lax.ppermute(held, "core", swap)
    held, x_held = lax.optimization_barrier((held, x_held))
    above = lax.ppermute(held, "y", minus)
    mix = jnp.where(
        xh == 0, jnp.concatenate([mine, theirs], 1), jnp.concatenate([theirs, mine], 1)
    )
    mix = jnp.broadcast_to(mix[:, :, None], (EXPERTS, 2 * TOK, 128))
    place, mix, tab = lax.optimization_barrier((place, mix, tab))
    here = assemble([w0], "pieces_here")
    above, from_x, from_z, here = lax.optimization_barrier((above, from_x, from_z, here))

    diagonal = [along_x(jnp.stack([from_z[0][1 - i], from_z[1][1 - i]]), i) for i in range(2)]
    below, far = lax.ppermute(held, "y", plus), lax.ppermute(above, "y", minus)
    ws = [here, assemble(from_z, "pieces_z"), assemble(from_x, "pieces_x")]
    below, above, ws = lax.optimization_barrier((below, above, ws))
    x_below, x_above = lax.ppermute(below, "core", swap), lax.ppermute(above, "core", swap)
    diagonal, far = lax.optimization_barrier((diagonal, far))
    x_far = lax.ppermute(far, "core", swap)
    ws.append(assemble(diagonal, "pieces_diagonal"))
    xs = [held, above, far, below, x_held, x_above, x_far, x_below]

    hbm, anywhere = pl.BlockSpec(memory_space=pltpu.HBM), pl.BlockSpec(memory_space=pl.ANY)
    sums = jax.ShapeDtypeStruct((16, 192, TOK), bf16)
    hidden = jax.ShapeDtypeStruct((2 * TOK, EXPERTS * 256), bf16)
    down_half = jax.ShapeDtypeStruct((4, 2, 192, EXPERTS * 256), bf16)
    dma = pltpu.SemaphoreType.DMA
    stage = pltpu.VMEM((2, 768, 2 * TOK), bf16)
    send, hidden, down_own = pl.pallas_call(
        hidden_kernel,
        out_shape=[sums, hidden, down_half],
        in_specs=[smem] + [hbm] * 13,
        out_specs=[hbm, vmem, vmem],
        scratch_shapes=[
            pltpu.VMEM((2 * TOK, 2 * HALF), bf16),
            pltpu.VMEM((EXPERTS, 2, 4, 2, 192, 256), bf16),
            pltpu.VMEM(down_half.shape, bf16),
            stage,
            pltpu.VMEM((EXPERTS, 2 * TOK, 128), f32),
            dma((8,)),
            dma((EXPERTS,)),
            dma((2,)),
            dma((2,)),
            dma,
        ],
        compiler_params=pltpu.CompilerParams(vmem_limit_bytes=34 * 2**20),
        name="hidden",
    )(tab, *xs, *ws, mix)
    other = lax.ppermute(send, "core", swap)
    own_sum = pl.pallas_call(
        own_kernel,
        out_shape=sums,
        in_specs=[vmem] * 2,
        out_specs=anywhere,
        scratch_shapes=[stage, dma((2,))],
        compiler_params=pltpu.CompilerParams(vmem_limit_bytes=24 * 2**20),
        cost_estimate=pl.CostEstimate(flops=2 * HALF * 2 * TOK * 1024, bytes_accessed=8 * 2**20, transcendentals=0),
        name="own_side",
    )(down_own, hidden)
    both = (own_sum.astype(f32) + other.astype(f32)).astype(bf16)
    parts = lax.all_to_all(both, chips, 0, 0)
    total = jnp.sum(parts.astype(f32), axis=0).astype(bf16)
    total = total.reshape(4, ROWS, TOK)[:, :45].reshape(180, 4, 128)
    return total.transpose(1, 2, 0)


def solution(mesh):
    fine = Mesh(mesh.devices.reshape(2, 2, 2, 2, 4, 2), ("zl", "xh", "xl", "zh", "y", "core"))
    grp, tp = ("zl", "xh", "xl"), ("zh", "y", "core")
    state = P(grp, tp, None, None)
    return jax.shard_map(
        shards,
        mesh=fine,
        in_specs=(state, state, state, state, P(), P(None, grp, tp), P(None, grp, None), P(None, grp, None)),
        out_specs=P(None, grp, tp),
        check_vma=False,
    )
```

```python
import functools

import jax
import jax.numpy as jnp
from jax import lax
from jax.experimental import pallas as pl
from jax.experimental.pallas import tpu as pltpu
from jax.sharding import Mesh
from jax.sharding import PartitionSpec as P

EXPERTS = 4
ROWS = 48
PART = 56
TOK = 512
HALF = 1536

learn_rate = 0.003
beta_one = 0.9
beta_two = 0.999
adam_eps = 1e-08
decay_rate = 0.1
bias_one = 1.0 - 0.9**20
bias_two = 1.0 - 0.999**20

bf16 = jnp.bfloat16
f32 = jnp.float32


def roll(x, by):
    if isinstance(by, int):
        by = by % 128
        if by == 0:
            return x
    return pltpu.roll(x, by, 1)


def pack_kernel(place, w_ref, o_ref):
    xl, zl = place[0], place[1]
    lane = lax.broadcasted_iota(jnp.int32, (ROWS, 128), 1)
    lane8 = lax.broadcasted_iota(jnp.int32, (8, 128), 1)
    within = lane % 64

    @pl.loop(0, 8)
    def _(k):
        def tile(s, kind, j):
            return w_ref[s, kind, :, pl.ds(pl.multiple_of(k * 384 + j * 128, 128), 128)].astype(f32)

        for i in range(16):
            a, off = (24 * i) // 128, (24 * i) % 128

            def source(s, kind):
                if off <= 104:
                    return tile(s, kind, a)
                return jnp.where(lane >= off, tile(s, kind, a), tile(s, kind, a + 1))

            pair = 2 * k + i // 8
            link_x, link_z = pair // 4, pair % 4
            jx, jz = (link_x + xl) % 2, (link_z + zl) % 2
            x_to, z_to = (link_x + jx) % 4, (link_z + jz) % 4
            to = (x_to // 2) * 16 + (z_to // 2) * 8 + i % 8
            halves, fold = [], jnp.zeros((8, 128), f32)
            for s in range(2):
                gate, up, down = source(s, 0), source(s, 1), source(s, 2)
                half = 64 * ((s + i // 8) % 2)
                gate, up = roll(gate, half - off), roll(up, half + 24 - off)
                main_down = roll(down, half + 48 - off)
                halves.append(jnp.where(within < 24, gate, jnp.where(within < 48, up, main_down)))
                for g in range(6):
                    at = 16 * g + 8 * s
                    rest = roll(down[8 * g : 8 * g + 8], at - off - 16)
                    fold = jnp.where((lane8 >= at) & (lane8 < at + 8), rest, fold)
            main = jnp.where(lane < 64, halves[i // 8], halves[1 - i // 8])
            o_ref[to, 2 * jx + jz] = jnp.concatenate([main, fold], 0).astype(bf16)


def assemble_kernel(along_x, place, *refs):
    *parts, o_ref = refs
    if len(parts) == 1:
        part = [lambda src, m=m: parts[0][src, m] for m in range(4)]
    elif along_x:
        part = [lambda src, m=m: parts[m // 2][m % 2, src] for m in range(4)]
    else:
        part = [lambda src, m=m: parts[m % 2][m // 2, src] for m in range(4)]
    lane = lax.broadcasted_iota(jnp.int32, (ROWS, 128), 1)
    lane8 = lax.broadcasted_iota(jnp.int32, (8, 128), 1)

    for zl in range(2):

        @pl.when(place[1] == zl)
        def _():
            @pl.loop(0, 32)
            def _(src):
                chunk = src % 16
                side = (chunk // 4 + place[2]) % 2
                row = (2 * side + chunk // 8) * 192 + (chunk % 4) * ROWS
                row = pl.ds(pl.multiple_of(row, ROWS), ROWS)
                loaded = [part[m](src).astype(f32) for m in range(4)]
                for slot in range(2):
                    swap = slot ^ zl
                    for pair in range(2):
                        first, second = loaded[2 * pair], loaded[2 * pair + 1]
                        main = roll(jnp.where((lane // 64) == swap, first[:ROWS], second[:ROWS]), swap * 64)
                        rows = []
                        for g in range(6):
                            at = 16 * g + 8 * slot
                            low, high = roll(second[ROWS:], -at), roll(first[ROWS:], 64 - at)
                            cur = main[8 * g : 8 * g + 8]
                            rows.append(jnp.where(lane8 < 8, low, jnp.where((lane8 // 8) == 8, high, cur)))
                        col = slice(pair * 128, pair * 128 + 128)
                        piece = (src // 16) * 2 + slot
                        o_ref[0, piece, row, col] = main.astype(bf16)
                        o_ref[1, piece, row, col] = jnp.concatenate(rows, 0).astype(bf16)


def fetch_pieces(tab, ws, use, experts, start):
    @pl.loop(4 * experts[0], 4 * experts[1])
    def _(i):
        src, slot = tab[2 * i], tab[2 * i + 1]
        for relation in range(4):

            @pl.when(src // 2 == relation)
            def _():
                start(i // 4, i % 4, ws[relation].at[use, (src % 2) * 2 + slot])


def wait_all(ref, sem):
    pltpu.make_async_copy(ref, ref, sem).wait()


def fetch_down(tab, ws, wd, dsem, side):
    def start(e, b, block):
        to = wd.at[pl.ds(2 * (b % 2), 2), b // 2, :, pl.ds(pl.multiple_of(e * 256, 256), 256)]
        pltpu.make_async_copy(block.at[side], to, dsem).start()

    fetch_pieces(tab, ws, 1, (0, EXPERTS), start)


def down(wd, hid, stage, osem, out_ref):
    for n in range(2):
        rows = wd[2 * n : 2 * n + 2].reshape(768, EXPERTS * 256)
        out = lax.dot_general(rows, hid[...], (((1,), (1,)), ((), ())), preferred_element_type=f32)
        stage[n] = out.astype(bf16)
        for q in range(4):
            for z in range(2):
                at = 8 * z + 4 * (q % 2) + 2 * n + q // 2
                block = stage.at[n, pl.ds(q * 192, 192), pl.ds(z * TOK, TOK)]
                pltpu.make_async_copy(block, out_ref.at[at], osem.at[n]).start()
    for n in range(2):
        wait_all(stage.at[n], osem.at[n])


def hidden_kernel(tab, *refs):
    xs, ws, mix_ref, (send_ref, hid, wd_own) = refs[:8], refs[8:12], refs[12], refs[13:16]
    x, wg, wd, stage, mix, xsem, gsem, dsem, osem, msem = refs[16:]
    y = tab[32]

    def start(e, b, block):
        to = wg.at[e, :, pl.ds(2 * (b % 2), 2), b // 2]
        pltpu.make_async_copy(block, to, gsem.at[e]).start()

    gets = []
    for side in range(2):
        for n, ref in enumerate(xs[4 * side : 4 * side + 4]):
            lanes = pl.ds(pl.multiple_of(side * HALF + ((y + n) % 4) * 384, 128), 384)
            gets.append(pltpu.make_async_copy(ref, x.at[:, lanes], xsem.at[len(gets)]))
            gets[-1].start()
    fetch_pieces(tab, ws, 0, (0, 1), start)
    get_mix = pltpu.make_async_copy(mix_ref, mix, msem)
    for get in gets:
        get.wait()
    get_mix.start()
    fetch_pieces(tab, ws, 0, (1, EXPERTS), start)
    fetch_down(tab, ws, wd, dsem.at[1], 1)
    fetch_down(tab, ws, wd_own, dsem.at[0], 0)
    get_mix.wait()

    lanes = lax.broadcasted_iota(jnp.int32, (2 * TOK, 128), 1) % 64

    @pl.loop(0, EXPERTS)
    def _(e):
        wait_all(wg.at[e], gsem.at[e])
        acc = jnp.dot(x[...], wg[e].reshape(2 * HALF, 256), preferred_element_type=f32)
        for n in range(2):
            gate = acc[:, n * 128 : (n + 1) * 128]
            hidden = (pltpu.roll(gate, 104, 1) + 1.0) * gate * jax.nn.sigmoid(1.702 * gate)
            hidden = hidden.astype(bf16).astype(f32) * mix[e]
            hidden = jnp.where((lanes >= 48) | (lanes < 8), pltpu.roll(hidden, 48, 1), 0.0)
            hid[:, pl.ds(pl.multiple_of(e * 256 + n * 128, 128), 128)] = hidden.astype(bf16)

    wait_all(wd, dsem.at[1])
    down(wd, hid, stage, osem, send_ref)
    wait_all(wd_own, dsem.at[0])


def own_kernel(wd, hid, own_ref, stage, osem):
    down(wd, hid, stage, osem, own_ref)


def update(master, moment_one, moment_two, gradient):
    moment_new = beta_one * moment_one + (1.0 - beta_one) * gradient
    second_new = beta_two * moment_two + (1.0 - beta_two) * gradient * gradient
    adjust = (
        moment_new / bias_one / (jnp.sqrt(second_new / bias_two) + adam_eps) + decay_rate * master
    )
    updated = (master - learn_rate * adjust).astype(bf16)
    return jnp.pad(updated.transpose(0, 2, 1, 3), ((0, 0), (0, 0), (0, ROWS - 45), (0, 3072 - 2880)))


def shards(master, moment_one, moment_two, gradient, piece_owner, tokens, routes, mix_weight):
    xl, zl, core = lax.axis_index("xl"), lax.axis_index("zl"), lax.axis_index("core")
    chips = ("xh", "zh", "y")
    swap = ((0, 1), (1, 0))
    plus = [(i, (i + 1) % 4) for i in range(4)]
    minus = [(i, (i - 1) % 4) for i in range(4)]

    own_x = tokens.transpose(2, 0, 1).reshape(4, 45, TOK)
    own_x = jnp.pad(own_x, ((0, 0), (0, ROWS - 45), (0, 0))).reshape(4 * ROWS, TOK)
    xh, zh = lax.axis_index("xh"), lax.axis_index("zh")
    at_z, at_x = lax.ppermute(own_x, "zh", swap), lax.ppermute(own_x, "xh", swap)
    def in_order(first, here, other):
        return jnp.stack([jnp.where(first, here, other), jnp.where(first, other, here)])


    flat_routes = routes.reshape(TOK, 2)
    flat_mix = mix_weight.reshape(TOK, 2)
    mine = jnp.sum(
        jnp.where(flat_routes[None] == jnp.arange(EXPERTS, dtype=jnp.int32)[:, None, None], flat_mix[None], 0.0), axis=2
    )
    updated = update(master, moment_one, moment_two, gradient)
    updated, at_x, mine = lax.optimization_barrier((updated, at_x, mine))
    swapped = own_x, at_z, at_x, lax.ppermute(at_x, "zh", swap)
    theirs = lax.ppermute(mine, "xh", swap)

    inverse = jnp.zeros((16,), jnp.int32).at[piece_owner].set(jnp.arange(16, dtype=jnp.int32))
    grp = inverse // 2
    relation = ((grp % 2) ^ xl) * 2 + ((grp // 4) ^ zl)
    source = relation * 2 + (grp % 4) // 2
    tab = jnp.concatenate([jnp.stack([source, inverse % 2], 1).reshape(-1), lax.axis_index("y").reshape(1)]).astype(jnp.int32)
    place = jnp.stack([xl, zl, core]).astype(jnp.int32)

    smem, vmem = pl.BlockSpec(memory_space=pltpu.SMEM), pl.BlockSpec(memory_space=pltpu.VMEM)
    packed = pl.pallas_call(
        pack_kernel,
        out_shape=jax.ShapeDtypeStruct((32, 4, PART, 128), bf16),
        in_specs=[smem, vmem],
        out_specs=vmem,
        compiler_params=pltpu.CompilerParams(vmem_limit_bytes=16 * 2**20),
        name="pack",
    )(place, updated)
    packed, swapped, theirs = lax.optimization_barrier((packed, swapped, theirs))
    w0 = lax.all_to_all(packed, ("xh", "zh", "y", "core"), 0, 0)
    held = in_order(xh == 0, in_order(zh == 0, *swapped[:2]), in_order(zh == 0, *swapped[2:]))
    held = held.transpose(0, 3, 1, 2).reshape(2 * TOK, 384)

    ax, az = ("xh", "xl"), ("zl", "zh")
    plus_z = [((i % 2) * 2 + i // 2, (j % 2) * 2 + j // 2) for i, j in plus]
    minus_z = [(j, i) for i, j in plus_z]

    def along_x(block, i):
        return lax.ppermute(block, ax, plus if i else minus)

    def along_z(block, j):
        return lax.ppermute(block, az, plus_z if j else minus_z)

    grid = w0.reshape(32, 2, 2, PART, 128)
    from_x = [along_x(jnp.swapaxes(grid[:, 1 - i], 0, 1), i) for i in range(2)]
    from_z = [along_z(jnp.swapaxes(grid[:, :, 1 - j], 0, 1), j) for j in range(2)]

    def assemble(parts, name):
        return pl.pallas_call(
            functools.partial(assemble_kernel, name != "pieces_z"),
            out_shape=jax.ShapeDtypeStruct((2, 4, 768, 256), bf16),
            in_specs=[smem] + [vmem] * len(parts),
            out_specs=vmem,
            compiler_params=pltpu.CompilerParams(vmem_limit_bytes=16 * 2**20),
            cost_estimate=pl.CostEstimate(flops=0, bytes_accessed=16 * 2**20, transcendentals=0),
            name=name,
        )(place, *parts).reshape(2, 4, 2, 2, 192, 256)

    x_held = lax.ppermute(held, "core", swap)
    held, x_held = lax.optimization_barrier((held, x_held))
    above = lax.ppermute(held, "y", minus)
    mix = jnp.where(
        xh == 0, jnp.concatenate([mine, theirs], 1), jnp.concatenate([theirs, mine], 1)
    )
    mix = jnp.broadcast_to(mix[:, :, None], (EXPERTS, 2 * TOK, 128))
    place, mix, tab = lax.optimization_barrier((place, mix, tab))
    here = assemble([w0], "pieces_here")
    above, from_x, from_z, here = lax.optimization_barrier((above, from_x, from_z, here))

    diagonal = [along_x(jnp.stack([from_z[0][1 - i], from_z[1][1 - i]]), i) for i in range(2)]
    below, far = lax.ppermute(held, "y", plus), lax.ppermute(above, "y", minus)
    ws = [here, assemble(from_z, "pieces_z"), assemble(from_x, "pieces_x")]
    below, above, ws = lax.optimization_barrier((below, above, ws))
    x_below, x_above = lax.ppermute(below, "core", swap), lax.ppermute(above, "core", swap)
    diagonal, far = lax.optimization_barrier((diagonal, far))
    x_far = lax.ppermute(far, "core", swap)
    ws.append(assemble(diagonal, "pieces_diagonal"))
    xs = [held, above, far, below, x_held, x_above, x_far, x_below]

    hbm, anywhere = pl.BlockSpec(memory_space=pltpu.HBM), pl.BlockSpec(memory_space=pl.ANY)
    sums = jax.ShapeDtypeStruct((16, 192, TOK), bf16)
    hidden = jax.ShapeDtypeStruct((2 * TOK, EXPERTS * 256), bf16)
    down_half = jax.ShapeDtypeStruct((4, 2, 192, EXPERTS * 256), bf16)
    dma = pltpu.SemaphoreType.DMA
    stage = pltpu.VMEM((2, 768, 2 * TOK), bf16)
    send, hidden, down_own = pl.pallas_call(
        hidden_kernel,
        out_shape=[sums, hidden, down_half],
        in_specs=[smem] + [hbm] * 13,
        out_specs=[hbm, vmem, vmem],
        scratch_shapes=[
            pltpu.VMEM((2 * TOK, 2 * HALF), bf16),
            pltpu.VMEM((EXPERTS, 2, 4, 2, 192, 256), bf16),
            pltpu.VMEM(down_half.shape, bf16),
            stage,
            pltpu.VMEM((EXPERTS, 2 * TOK, 128), f32),
            dma((8,)),
            dma((EXPERTS,)),
            dma((2,)),
            dma((2,)),
            dma,
        ],
        compiler_params=pltpu.CompilerParams(vmem_limit_bytes=34 * 2**20),
        name="hidden",
    )(tab, *xs, *ws, mix)
    other = lax.ppermute(send, "core", swap)
    own_sum = pl.pallas_call(
        own_kernel,
        out_shape=sums,
        in_specs=[vmem] * 2,
        out_specs=anywhere,
        scratch_shapes=[stage, dma((2,))],
        compiler_params=pltpu.CompilerParams(vmem_limit_bytes=24 * 2**20),
        cost_estimate=pl.CostEstimate(flops=2 * HALF * 2 * TOK * 1024, bytes_accessed=8 * 2**20, transcendentals=0),
        name="own_side",
    )(down_own, hidden)
    both = (own_sum.astype(f32) + other.astype(f32)).astype(bf16)
    parts = lax.all_to_all(both, chips, 0, 0)
    total = jnp.sum(parts.astype(f32), axis=0).astype(bf16)
    total = total.reshape(4, ROWS, TOK)[:, :45].reshape(180, 4, 128)
    return total.transpose(1, 2, 0)


def solution(mesh):
    fine = Mesh(mesh.devices.reshape(2, 2, 2, 2, 4, 2), ("zl", "xh", "xl", "zh", "y", "core"))
    grp, tp = ("zl", "xh", "xl"), ("zh", "y", "core")
    state = P(grp, tp, None, None)
    return jax.shard_map(
        shards,
        mesh=fine,
        in_specs=(state, state, state, state, P(), P(None, grp, tp), P(None, grp, None), P(None, grp, None)),
        out_specs=P(None, grp, tp),
        check_vma=False,
    )
```
